32 devices in a mesh: chan: 8 (over z, core), tile: 4 (over y, x).
Axes of the slice: x: 2, y: 2, z: 4, core: 2. Of those that a mesh axis runs over, the one named last changes fastest.
Arguments:
- residual: float32 [8, 2048, 2048], P('chan', 'tile'), may hold values from -24 to 24
- direction: float32 [8, 2048, 2048], P('chan', 'tile'), may hold values from -24 to 24
- cover: int32 [8, 4, 4, 1], P('chan', 'tile'), may hold values from 0 to 256, as said below
- kernels: bfloat16 [8, 4, 4, 1, 8192], P('chan', 'tile'), may hold values from -0.75 to 0.75
- weights: bfloat16 [8, 4, 4, 1, 4096], P('chan', 'tile'), may hold values from 0.5 to 5
- spectrum: float32 [8, 2, 2048], P('chan'), may hold values from 0.2 to 2
Outputs:
- new_residual: float32 [8, 2048, 2048], P('chan', 'tile')
- new_direction: float32 [8, 2048, 2048], P('chan', 'tile')
The draws below stay inside these ranges and needn't reach their ends.
Inputs may be any that keep to these rules, and one draw needn't show every extreme that they name: cover[c, o, w, j] names one of the 256 uv tiles of device o of tile, numbered row by row over its tile columns, on which slot j of device w's subgrids lands; the value 256 marks an empty slot. Several slots may name one tile.
All inputs are finite; a program needn't handle non-finite values.
Results may differ from the reference program's by a relative error of at most 0.0013.
Values may be sent and summed in bfloat16 or wider, within the bound.
A program may use at most 128 MiB of HBM per device.

```python
import math
import jax
import jax.numpy as jnp
from jax import lax

NI = 2048
SUB = 64
Q = 64
CAP = 1
CHANNELS = 8
TCOL = 8
TLOC = 256
N_TILE = 4


def smooth_part(key, center, amp_lo, amp_hi):
    rows = jnp.arange(NI, dtype=jnp.int32)[None, :, None]
    cols = jnp.arange(NI, dtype=jnp.int32)[None, None, :]
    total = jnp.full((CHANNELS, NI, NI), center, jnp.float32)
    for mode in range(3):
        mode_key = jax.random.fold_in(key, 100 + mode)
        freq_v = jax.random.randint(jax.random.fold_in(mode_key, 1), (CHANNELS, 1, 1), 0, 4)
        freq_u = jax.random.randint(jax.random.fold_in(mode_key, 2), (CHANNELS, 1, 1), 0, 4)
        phase = jax.random.uniform(jax.random.fold_in(mode_key, 3), (CHANNELS, 1, 1), jnp.float32, -math.pi, math.pi)
        amplitude = jax.random.uniform(jax.random.fold_in(mode_key, 4), (CHANNELS, 1, 1), jnp.float32, amp_lo, amp_hi)
        turns = ((freq_v * rows + freq_u * cols) % NI).astype(jnp.float32)
        total = total + amplitude * jnp.cos(2.0 * math.pi / NI * turns + phase)
    return total


def field_law(key):
    shape = (CHANNELS, NI, NI)
    chan_pos = jnp.arange(CHANNELS, dtype=jnp.float32)[:, None, None] / max(CHANNELS - 1, 1)
    row_pos = jnp.arange(NI, dtype=jnp.float32)[None, :, None] / (NI - 1)
    rough = 0.5 * jnp.clip(jax.random.normal(key, shape, jnp.float32), -5.0, 5.0)
    smooth = smooth_part(jax.random.fold_in(key, 7), 1.2, 0.25, 0.7)
    return (rough + smooth) * jnp.exp(math.log(2.0) * (chan_pos + row_pos))


def draw_residual(key, part):
    return field_law(jax.random.fold_in(key, 11))


def draw_direction(key, part):
    return 0.75 * field_law(jax.random.fold_in(key, 11)) + 0.25 * field_law(jax.random.fold_in(key, 23))


def draw_cover(key, part):
    shape = (CHANNELS, N_TILE, N_TILE, CAP)
    owner = jnp.arange(N_TILE, dtype=jnp.int32)[None, :, None, None]
    distance = jnp.minimum(owner, N_TILE - 1 - owner)
    threshold = jnp.maximum(2, 8 - 2 * distance)
    chance = jax.random.randint(jax.random.fold_in(key, 1), shape, 0, 8)
    tiles = jax.random.randint(jax.random.fold_in(key, 2), shape, 0, TLOC)
    chosen = jnp.where(chance < threshold, tiles, TLOC)
    chosen = chosen.at[:, 0, 0, 0].set(0)
    return chosen.at[:, N_TILE // 2, 0, CAP - 1].set(TLOC)


def level_of(key, shape, pieces, least, high):
    def one(dim, parts):
        draws = jax.random.uniform(jax.random.fold_in(jax.random.fold_in(key, 6), dim), (parts,), jnp.float32, least / len(pieces), high / len(pieces))
        return jnp.repeat(jnp.exp(draws), shape[dim] // parts).reshape((-1,) + (1,) * (len(shape) - dim - 1))

    loudness = one(*pieces[0])
    for cut in pieces[1:]:
        loudness = loudness * one(*cut)
    return loudness


def bell_draw(own_key, shape, spread, reach, split=(), held_as=jnp.bfloat16):
    array = jax.random.normal(own_key, shape, jnp.float32) * spread
    if len(split) > 0:
        array = level_of(own_key, shape, split, -0.22, 0.18) * array
    return jnp.clip(array, min=-reach, max=reach).astype(held_as)


def setup_inputs(seed: int = 0) -> dict:
    streams_of = jax.random.split(jax.random.key(seed), 7)
    return {
        "residual": draw_residual(jax.random.fold_in(streams_of[6], 71), 0),
        "direction": draw_direction(jax.random.fold_in(streams_of[6], 71), 0),
        "cover": draw_cover(jax.random.fold_in(streams_of[6], 71), 0),
        "kernels": bell_draw(streams_of[3], (CHANNELS, N_TILE, N_TILE, CAP, 2 * Q * SUB), SUB ** -0.5, 0.75, ((0, 8), (1, 4))),
        "weights": jnp.clip(jnp.exp(math.log(5.0) - 2.3025851 * jax.random.uniform(streams_of[4], (CHANNELS, N_TILE, N_TILE, CAP, Q * Q), jnp.float32) ** level_of(streams_of[4], (CHANNELS, N_TILE, N_TILE, CAP, Q * Q), ((0, 8), (1, 4)), -0.2, 0.2)), 0.5, 5.0).astype(jnp.bfloat16),
        "spectrum": jnp.clip(jnp.exp(math.log(2.0) - 2.3025851 * jax.random.uniform(streams_of[5], (CHANNELS, 2, NI), jnp.float32) ** level_of(streams_of[5], (CHANNELS, 2, NI), ((0, 8),), -0.2, 0.2)), 0.2, 2.0),
    }


def regrid_slots(patch, kern_v, kern_u, noise):
    highest = lax.Precision.HIGHEST
    first = jnp.einsum("mqv,cmvu->cmqu", kern_v, patch, precision=highest)
    sampled = jnp.einsum("cmqu,mru->cmqr", first, kern_u, precision=highest) * noise[None]
    second = jnp.einsum("mqv,cmqr->cmvr", kern_v, sampled, precision=highest)
    return jnp.einsum("cmvr,mru->cmvu", second, kern_u, precision=highest)


def channel_image(inputs):
    field, cov, kern, noise, spec = inputs
    ftype = field.dtype
    grid = jnp.fft.fft2(field)
    tile_rows = NI // SUB
    tile_cols = NI // SUB
    grid_re = jnp.real(grid).astype(ftype)
    grid_im = jnp.imag(grid).astype(ftype)

    def to_tiles(values):
        return values.reshape(tile_rows, SUB, tile_cols, SUB).transpose(0, 2, 1, 3).reshape(tile_rows * tile_cols, SUB, SUB)

    owner = jnp.arange(N_TILE, dtype=jnp.int32)[:, None, None]
    safe = jnp.minimum(cov, TLOC - 1)
    global_index = (safe // TCOL) * tile_cols + owner * TCOL + safe % TCOL
    live = (cov < TLOC).astype(ftype).reshape(-1)
    flat_index = global_index.reshape(-1).astype(jnp.int32)
    tiles = jnp.stack([to_tiles(grid_re), to_tiles(grid_im)])
    patch = tiles[:, flat_index] * live[None, :, None, None]
    kern_ow = jnp.swapaxes(kern, 0, 1).astype(ftype).reshape(-1, 2 * Q * SUB)
    kern_v = kern_ow[:, :Q * SUB].reshape(-1, Q, SUB)
    kern_u = kern_ow[:, Q * SUB:].reshape(-1, Q, SUB)
    noise_ow = jnp.swapaxes(noise, 0, 1).astype(ftype).reshape(-1, Q, Q)
    result = regrid_slots(patch, kern_v, kern_u, noise_ow) * live[None, :, None, None]
    summed = jnp.zeros((2, tile_rows * tile_cols, SUB, SUB), ftype).at[:, flat_index].add(result)
    summed = summed.reshape(2, tile_rows, tile_cols, SUB, SUB).transpose(0, 1, 3, 2, 4).reshape(2, NI, NI)
    prior = spec[0][:, None] * spec[1][None, :]
    gridded = lax.complex(summed[0] + prior * grid_re, summed[1] + prior * grid_im)
    return jnp.real(jnp.fft.ifft2(gridded)).astype(ftype)


def reference(residual, direction, cover, kernels, weights, spectrum):
    image = lax.map(channel_image, (direction, cover, kernels, weights, spectrum))
    total_rr = jnp.sum(residual * residual)
    curvature = jnp.sum(direction * image)
    alpha = total_rr / curvature
    new_residual = residual - alpha * image
    fresh = jnp.sum(new_residual * new_residual)
    new_direction = new_residual + (fresh / total_rr) * direction
    return new_residual, new_direction
```

```python
import math

import jax
import jax.numpy as jnp
import numpy as np
from jax import lax
from jax.sharding import PartitionSpec as P

SUB = 64
Q = 64
RADIX = 8
HIGH = lax.Precision.HIGH
ROOT = 0.5**0.5


def phase_table(left, right, length):
    angle = 2.0 * math.pi / length * (np.outer(left, right) % length)
    return np.cos(angle), np.sin(angle)


def full_tables(length):
    part = length // RADIX
    index = np.arange(part)
    blocks = []
    for r in range(RADIX):
        co, si = phase_table(RADIX * index + r, index, length)
        blocks.append(np.block([[co, si], [-si, co]]))
    return np.stack(blocks).astype(np.float32)


def half_tables(length):
    part = length // RADIX
    index = np.arange(part)
    half = np.arange(part // 2)
    blocks = []
    for r in (0, RADIX // 2):
        co, si = phase_table(RADIX * half + r, index, length)
        low = -si
        if r == 0:
            low[0] = 1.0 - 2.0 * (index % 2)
        blocks.append(np.concatenate([co, low]))
    return np.stack(blocks).astype(np.float32)


def fold_real(x):
    s04, d04, s26, d26 = x[0] + x[4], x[0] - x[4], x[2] + x[6], x[2] - x[6]
    s15, d15, s37, d37 = x[1] + x[5], x[1] - x[5], x[3] + x[7], x[3] - x[7]
    even, odd = s04 + s26, s15 + s37
    minus, plus = (d15 - d37) * ROOT, (d15 + d37) * ROOT
    return (
        (even + odd, None),
        (d04 + minus, -d26 - plus),
        (s04 - s26, s37 - s15),
        (d04 - minus, d26 - plus),
        (even - odd, None),
    )


def fold_complex(re, im):
    left, right = fold_real(re), fold_real(im)
    out = [(left[0][0], right[0][0])]
    for r in (1, 2, 3):
        out.append((left[r][0] - right[r][1], left[r][1] + right[r][0]))
    out.append((left[4][0], right[4][0]))
    for r in (3, 2, 1):
        out.append((left[r][0] + right[r][1], right[r][0] - left[r][1]))
    return out


def unfold_real(z0, z4, z):
    (a1, b1), (a2, b2), (a3, b3) = z
    even, odd = z0 + z4, z0 - z4
    sa, da, sb, db = a1 + a3, a1 - a3, b1 + b3, b1 - b3
    return (
        even + sa + a2,
        odd + (da - sb) * ROOT - b2,
        even - db - a2,
        odd - (da + sb) * ROOT + b2,
        even - sa + a2,
        odd - (da - sb) * ROOT - b2,
        even + db - a2,
        odd + (da + sb) * ROOT + b2,
    )


def mirror(values):
    return jnp.roll(values[..., ::-1], 1, axis=-1)


def by_residue(values):
    return values.reshape(-1, RADIX).T


def body(residual, direction, cover, kernels, weights, spectrum):
    rows_now = residual[0]
    field = direction[0]
    devices = lax.axis_size("tile")
    me = lax.axis_index("tile")
    slab, length = field.shape
    part = length // RADIX
    columns = length // 2 // devices
    tile_cols = length // SUB // devices
    tile_count = (length // SUB) * tile_cols
    table = full_tables(length)
    small = half_tables(length)

    folded = fold_real([field[:, j * part : (j + 1) * part] for j in range(RADIX)])
    wide = jnp.stack([jnp.concatenate(folded[r], axis=-1) for r in (1, 2, 3)])
    lean = jnp.stack([folded[0][0], folded[4][0]])
    wide_out = jnp.einsum("ryp,rop->ryo", wide, table[1:4], precision=HIGH)
    lean_out = jnp.einsum("ryp,rop->ryo", lean, small, precision=HIGH)
    top = jnp.maximum(jnp.max(jnp.abs(field)), 1e-30) * 64.0
    tops = lax.all_gather(top, "tile")
    half = part // 2
    pair = jnp.stack(
        [
            jnp.concatenate(
                [wide_out[r][:, o * part : (o + 1) * part] for r in range(3)]
                + [lean_out[r][:, o * half : (o + 1) * half] for r in range(2)],
                axis=-1,
            )
            for o in range(2)
        ]
    )
    sent = (pair * (1.0 / top)).astype(jnp.float16)
    here = lax.all_to_all(sent, "tile", split_axis=2, concat_axis=1, tiled=True)

    listing = jnp.swapaxes(lax.all_gather(cover[0, 0], "tile"), 0, 1)
    count = listing.size
    group = count if devices <= 4 else count // devices
    owner = lax.broadcasted_iota(jnp.int32, listing.shape, 1)
    live = (listing < tile_count).astype(jnp.float32)
    safe = jnp.minimum(listing, tile_count - 1)
    tile_a = (safe // tile_cols).reshape(-1)
    tile_b = (owner * tile_cols + safe % tile_cols).reshape(-1)
    period = length // SUB

    def turn(index, position):
        angle = (2.0 * math.pi / period) * ((index[:, None] * position) % period).astype(jnp.float32)
        return jnp.cos(angle), jnp.sin(angle)

    steps = SUB // RADIX
    spots = np.arange(part)
    offset = (RADIX * np.arange(steps)[None, :] + np.arange(RADIX)[:, None]).reshape(-1)
    inner = phase_table(spots, offset, length)
    inner_re = inner[0].astype(np.float32).reshape(part, RADIX, steps).transpose(1, 0, 2)[:, :, None]
    inner_im = inner[1].astype(np.float32).reshape(part, RADIX, steps).transpose(1, 0, 2)[:, :, None]
    nought = jnp.zeros_like(lean[0])
    every = jnp.stack(
        [
            jnp.concatenate([lean[0], nought], axis=-1),
            wide[0],
            wide[1],
            wide[2],
            jnp.concatenate([lean[1], nought], axis=-1),
            jnp.concatenate([folded[3][0], -folded[3][1]], axis=-1),
            jnp.concatenate([folded[2][0], -folded[2][1]], axis=-1),
            jnp.concatenate([folded[1][0], -folded[1][1]], axis=-1),
        ]
    )
    rows_at = me * slab + jnp.arange(slab, dtype=jnp.int32)
    fine = (jnp.arange(SUB, dtype=jnp.int32)[:, None] * rows_at[None]) % length
    fine_angle = (2.0 * math.pi / length) * fine.astype(jnp.float32)
    fine_re, fine_im = jnp.cos(fine_angle)[None], jnp.sin(fine_angle)[None]

    def along_table(tile_b):
        base_re, base_im = turn(tile_b, jnp.arange(part, dtype=jnp.int32)[None])
        base_re, base_im = base_re.T[None, :, :, None], base_im.T[None, :, :, None]
        along_re = (inner_re * base_re - inner_im * base_im).reshape(RADIX, part, group * steps)
        along_im = (inner_re * base_im + inner_im * base_re).reshape(RADIX, part, group * steps)
        along = jnp.concatenate(
            [
                jnp.concatenate([along_re, -along_im], axis=-1),
                jnp.concatenate([along_im, along_re], axis=-1),
            ],
            axis=1,
        )
        return along

    def down_table(tile_a):
        step_re, step_im = turn(tile_a, rows_at[None])
        step_re, step_im = step_re[:, None], step_im[:, None]
        down_re = fine_re * step_re - fine_im * step_im
        down_im = fine_re * step_im + fine_im * step_re
        down = jnp.stack(
            [jnp.stack([down_re, down_im], axis=2), jnp.stack([-down_im, down_re], axis=2)], axis=1
        )
        return down

    def gather_patches(where):
        strip = jnp.einsum("ryp,rpo->ryo", every, along_table(where[1]), precision=HIGH)
        strip = strip.reshape(RADIX, slab, 2, group, steps)
        return jnp.einsum("movpy,rypmt->movtr", down_table(where[0]), strip, precision=HIGH)

    def scatter_patches(where, spread):
        lifted = jnp.einsum("movpy,movtr->rypmt", down_table(where[0]), spread, precision=HIGH)
        lifted = lifted.reshape(RADIX, slab, 2 * group * steps)
        return jnp.einsum("ryo,rpo->ryp", lifted, along_table(where[1]), precision=HIGH)

    places = (tile_a.reshape(-1, group), tile_b.reshape(-1, group))
    if group == count:
        partial = gather_patches((places[0][0], places[1][0]))
    else:
        partial = lax.map(gather_patches, places)
    partial = partial.reshape(devices, count // devices, 2, SUB, SUB)
    patch = lax.psum_scatter(partial, "tile", scatter_dimension=0, tiled=True)[0]
    own_live = live[me].reshape(-1)
    kern = kernels[0, 0].reshape(-1, 2 * Q * SUB).astype(jnp.float32)
    kern_v = kern[:, : Q * SUB].reshape(-1, Q, SUB)
    kern_u = kern[:, Q * SUB :].reshape(-1, Q, SUB)
    noise = weights[0, 0].reshape(-1, Q, Q).astype(jnp.float32) * own_live[:, None, None]
    section = jnp.einsum("mqv,mcvu->mcqu", kern_v, patch, precision=HIGH)
    sampled = jnp.einsum("mcqu,mru->mcqr", section, kern_u, precision=HIGH) * noise[:, None]
    again = jnp.einsum("mqv,mcqr->mcvr", kern_v, sampled, precision=HIGH)
    regridded = jnp.einsum("mcvr,mru->mcvu", again, kern_u, precision=HIGH)
    spread = lax.all_gather(regridded, "tile").reshape(-1, group, 2, SUB, steps, RADIX)
    if group == count:
        added = scatter_patches((places[0][0], places[1][0]), spread[0])
    else:
        added = lax.fori_loop(
            0,
            count // group,
            lambda i, sofar: sofar + scatter_patches((places[0][i], places[1][i]), spread[i]),
            jnp.zeros((RADIX, slab, 2 * part), jnp.float32),
        )

    scale = jnp.repeat(tops, slab)[None, :, None]
    here = (here.astype(jnp.float32) * scale).reshape(2, RADIX, part, columns)
    turned = fold_complex(list(here[0]), list(here[1]))
    turned = jnp.stack([jnp.concatenate(z, axis=0) for z in turned])
    grid = jnp.einsum("rop,rpu->rou", table, turned, precision=HIGH).reshape(RADIX, 2, part, columns)
    spec_v, spec_u = spectrum[0, 0], spectrum[0, 1]
    v_plus, v_minus = by_residue(spec_v), by_residue(mirror(spec_v))

    def to_list(values):
        rows = by_residue(values)
        return jnp.concatenate([rows[1], rows[2], rows[3], rows[0, :half], rows[4, :half]])

    edge = spec_u[0], spec_u[length // 2]
    packed = 3 * part
    flat = jnp.full((1,), (edge[0] + edge[1]) * 0.25)
    u_plus = lax.dynamic_update_slice(to_list(spec_u), flat, (packed,))
    u_minus = lax.dynamic_update_slice(to_list(mirror(spec_u)), flat, (packed,))
    u_plus = lax.dynamic_slice_in_dim(u_plus, me * columns, columns)
    u_minus = lax.dynamic_slice_in_dim(u_minus, me * columns, columns)
    prior = v_plus[:, :, None] * u_plus + v_minus[:, :, None] * u_minus
    spot = packed % columns
    lone = grid[:, :, :, spot]
    flip = jnp.concatenate([mirror(lone[:1]), lone[:0:-1, :, ::-1]])
    cross = (v_plus + v_minus) * ((edge[0] - edge[1]) * 0.25)
    flip = flip * cross[:, None] * jnp.array([1.0, -1.0], jnp.float32)[None, :, None]
    chosen = (jnp.arange(columns) == spot) & (me == packed // columns)
    gridded = grid * prior[:, None] + jnp.where(chosen, flip[..., None], 0.0)
    back = jnp.einsum(
        "rop,rou->rpu", table, gridded.reshape(RADIX, 2 * part, columns), precision=HIGH
    )
    back = fold_complex([back[r, :part] for r in range(RADIX)], [-back[r, part:] for r in range(RADIX)])
    column = jnp.stack(
        [jnp.concatenate([z[0] for z in back]), jnp.concatenate([-z[1] for z in back])]
    )
    crest = jnp.maximum(jnp.max(jnp.abs(column)), 1e-30) * (1.0 / 1024.0)
    crests = lax.all_gather(crest, "tile")
    reply = (column * (1.0 / crest)).astype(jnp.float16)
    line = lax.all_to_all(reply, "tile", split_axis=1, concat_axis=2, tiled=True)

    line = line.astype(jnp.float32) * jnp.repeat(crests, columns)[None, None]
    wide_in = jnp.stack(
        [jnp.concatenate([line[0, :, r * part : (r + 1) * part], line[1, :, r * part : (r + 1) * part]], axis=-1) for r in range(3)]
    )
    lean_in = jnp.stack(
        [
            jnp.concatenate([line[o, :, 3 * part + r * half : 3 * part + (r + 1) * half] for o in range(2)], axis=-1)
            for r in range(2)
        ]
    )
    wide_z = jnp.einsum("ryo,rop->ryp", wide_in, table[1:4], precision=HIGH)
    lean_z = jnp.einsum("ryo,rop->ryp", lean_in, small, precision=HIGH)
    z = []
    for r in (1, 2, 3):
        z.append(
            (
                wide_z[r - 1][:, :part] + added[r][:, :part] + added[RADIX - r][:, :part],
                wide_z[r - 1][:, part:] + added[r][:, part:] - added[RADIX - r][:, part:],
            )
        )
    lines = unfold_real(lean_z[0] + added[0][:, :part], lean_z[1] + added[4][:, :part], z)
    image = jnp.concatenate(lines, axis=-1) * (1.0 / float(length * length))

    own = jnp.stack(
        [
            jnp.sum(rows_now * rows_now),
            jnp.sum(field * image),
            jnp.sum(rows_now * image),
            jnp.sum(image * image),
        ]
    )
    total = lax.psum(own, ("chan", "tile"))
    alpha = total[0] / total[1]
    fresh = total[0] - 2.0 * alpha * total[2] + alpha * alpha * total[3]
    new_rows = rows_now - alpha * image
    new_field = new_rows + fresh / total[0] * field
    return (new_rows[None], new_field[None])


def solution(mesh):
    placed = (
        P("chan", "tile", None),
        P("chan", "tile", None),
        P("chan", "tile", None, None),
        P("chan", "tile", None, None, None),
        P("chan", "tile", None, None, None),
        P("chan", None, None),
    )
    return jax.shard_map(
        body,
        mesh=mesh,
        in_specs=placed,
        out_specs=(P("chan", "tile", None), P("chan", "tile", None)),
        check_vma=False,
    )
```

```python
import math

import jax
import jax.numpy as jnp
import numpy as np
from jax import lax
from jax.sharding import PartitionSpec as P

SUB = 64
Q = 64
RADIX = 8
HIGH = lax.Precision.HIGH
ROOT = 0.5**0.5


def phase_table(left, right, length):
    angle = 2.0 * math.pi / length * (np.outer(left, right) % length)
    return np.cos(angle), np.sin(angle)


def full_tables(length):
    part = length // RADIX
    index = np.arange(part)
    blocks = []
    for r in range(RADIX):
        co, si = phase_table(RADIX * index + r, index, length)
        blocks.append(np.block([[co, si], [-si, co]]))
    return np.stack(blocks).astype(np.float32)


def row_tables(length, table):
    part = length // RADIX
    index = np.arange(part)
    half = np.arange(part // 2)
    last = np.zeros((2, 2, part // 2, 2, part), np.float32)
    for place, r in enumerate((0, RADIX // 2)):
        co, si = phase_table(RADIX * half + r, index, length)
        low = -si
        if r == 0:
            low[0] = 1.0 - 2.0 * (index % 2)
        last[0, place, :, place] = co
        last[1, place, :, place] = low
    return np.concatenate([table[1:4], last.reshape(1, 2 * part, 2 * part)])


def fold_real(x):
    s04, d04, s26, d26 = x[0] + x[4], x[0] - x[4], x[2] + x[6], x[2] - x[6]
    s15, d15, s37, d37 = x[1] + x[5], x[1] - x[5], x[3] + x[7], x[3] - x[7]
    even, odd = s04 + s26, s15 + s37
    minus, plus = (d15 - d37) * ROOT, (d15 + d37) * ROOT
    return (
        (even + odd, None),
        (d04 + minus, -d26 - plus),
        (s04 - s26, s37 - s15),
        (d04 - minus, d26 - plus),
        (even - odd, None),
    )


def fold_complex(re, im):
    left, right = fold_real(re), fold_real(im)
    out = [(left[0][0], right[0][0])]
    for r in (1, 2, 3):
        out.append((left[r][0] - right[r][1], left[r][1] + right[r][0]))
    out.append((left[4][0], right[4][0]))
    for r in (3, 2, 1):
        out.append((left[r][0] + right[r][1], right[r][0] - left[r][1]))
    return out


def unfold_real(z0, z4, z):
    (a1, b1), (a2, b2), (a3, b3) = z
    even, odd = z0 + z4, z0 - z4
    sa, da, sb, db = a1 + a3, a1 - a3, b1 + b3, b1 - b3
    return (
        even + sa + a2,
        odd + (da - sb) * ROOT - b2,
        even - db - a2,
        odd - (da + sb) * ROOT + b2,
        even - sa + a2,
        odd - (da - sb) * ROOT - b2,
        even + db - a2,
        odd + (da + sb) * ROOT + b2,
    )


def mirror(values):
    return jnp.roll(values[..., ::-1], 1, axis=-1)


def by_residue(values):
    return values.reshape(-1, RADIX).T


def body(residual, direction, cover, kernels, weights, spectrum):
    rows_now = residual[0]
    field = direction[0]
    devices = lax.axis_size("tile")
    me = lax.axis_index("tile")
    slab, length = field.shape
    part = length // RADIX
    columns = length // 2 // devices
    tile_cols = length // SUB // devices
    tile_count = (length // SUB) * tile_cols
    table = full_tables(length)
    across = row_tables(length, table)

    folded = fold_real([field[:, j * part : (j + 1) * part] for j in range(RADIX)])
    rows = jnp.stack(
        [jnp.concatenate(folded[r], axis=-1) for r in (1, 2, 3)]
        + [jnp.concatenate([folded[0][0], folded[4][0]], axis=-1)]
    )
    top = jnp.maximum(jnp.max(jnp.abs(field)), 1e-30)
    listed = cover[0, 0].astype(jnp.float32).reshape(-1)
    facts = lax.all_gather(jnp.concatenate([listed, top[None]]), "tile")
    tops = facts[:, -1]
    sent = jnp.einsum("gyp,gop->gyo", rows, across, precision=HIGH)
    sent = (sent * (1.0 / (64.0 * top))).astype(jnp.float16)
    fine_split = devices // 4
    sent = sent.reshape(4, slab, 2, fine_split, columns).transpose(0, 3, 1, 2, 4)
    sent = sent.reshape(devices, slab, 2 * columns)
    here = lax.all_to_all(sent, "tile", split_axis=0, concat_axis=0, tiled=True)

    listing = jnp.swapaxes(facts[:, :-1].astype(jnp.int32).reshape((devices,) + cover.shape[2:]), 0, 1)
    count = listing.size
    group = count if devices <= 4 else count // devices
    owner = lax.broadcasted_iota(jnp.int32, listing.shape, 1)
    live = (listing < tile_count).astype(jnp.float32)
    safe = jnp.minimum(listing, tile_count - 1)
    tile_a = (safe // tile_cols).reshape(-1)
    tile_b = (owner * tile_cols + safe % tile_cols).reshape(-1)
    period = length // SUB

    def turn(index, position):
        angle = (2.0 * math.pi / period) * ((index[:, None] * position) % period).astype(jnp.float32)
        return jnp.cos(angle), jnp.sin(angle)

    steps = SUB // RADIX
    spots = np.arange(part)
    offset = (RADIX * np.arange(steps)[None, :] + np.arange(RADIX)[:, None]).reshape(-1)
    inner = phase_table(spots, offset, length)
    inner_re = inner[0].astype(np.float32).reshape(part, RADIX, steps).transpose(1, 0, 2)[:, :, None]
    inner_im = inner[1].astype(np.float32).reshape(part, RADIX, steps).transpose(1, 0, 2)[:, :, None]
    rows_at = me * slab + jnp.arange(slab, dtype=jnp.int32)
    fine = (jnp.arange(SUB, dtype=jnp.int32)[:, None] * rows_at[None]) % length
    fine_angle = (2.0 * math.pi / length) * fine.astype(jnp.float32)
    fine_re, fine_im = jnp.cos(fine_angle)[None], jnp.sin(fine_angle)[None]

    def along_table(tile_b):
        base_re, base_im = turn(tile_b, jnp.arange(part, dtype=jnp.int32)[None])
        base_re, base_im = base_re.T[None, :, :, None], base_im.T[None, :, :, None]
        along_re = (inner_re * base_re - inner_im * base_im).reshape(RADIX, part, group * steps)
        along_im = (inner_re * base_im + inner_im * base_re).reshape(RADIX, part, group * steps)
        nought = jnp.zeros_like(along_re[0])

        def block(first, second, turned):
            sign = -1.0 if turned else 1.0
            upper = jnp.concatenate([first, -second], axis=-1)
            return jnp.concatenate([upper, sign * jnp.concatenate([second, first], axis=-1)])

        groups = []
        for r in (1, 2, 3):
            s = RADIX - r
            groups.append(
                jnp.concatenate(
                    [block(along_re[r], along_im[r], False), block(along_re[s], along_im[s], True)],
                    axis=-1,
                )
            )
        upper = jnp.concatenate([along_re[0], -along_im[0], nought, nought], axis=-1)
        lower = jnp.concatenate([nought, nought, along_re[4], -along_im[4]], axis=-1)
        groups.append(jnp.concatenate([upper, lower]))
        return jnp.stack(groups)

    def down_table(tile_a):
        step_re, step_im = turn(tile_a, rows_at[None])
        step_re, step_im = step_re[:, None], step_im[:, None]
        down_re = fine_re * step_re - fine_im * step_im
        down_im = fine_re * step_im + fine_im * step_re
        down = jnp.stack(
            [jnp.stack([down_re, down_im], axis=2), jnp.stack([-down_im, down_re], axis=2)], axis=1
        )
        return down

    def gather_patches(where):
        strip = jnp.einsum("gyp,gpo->gyo", rows, along_table(where[1]), precision=HIGH)
        strip = strip.reshape(4, slab, 2, 2, group, steps)
        return jnp.einsum("movpy,gyhpmt->movhgt", down_table(where[0]), strip, precision=HIGH)

    def scatter_patches(where, spread):
        lifted = jnp.einsum("movpy,movhgt->gyhpmt", down_table(where[0]), spread, precision=HIGH)
        lifted = lifted.reshape(4, slab, 4 * group * steps)
        return jnp.einsum("gyo,gpo->gyp", lifted, along_table(where[1]), precision=HIGH)

    places = (tile_a.reshape(-1, group), tile_b.reshape(-1, group))
    if group == count:
        partial = gather_patches((places[0][0], places[1][0]))
    else:
        partial = lax.map(gather_patches, places)
    partial = partial.reshape(devices, count // devices, 2, SUB, SUB)
    patch = lax.psum_scatter(partial, "tile", scatter_dimension=0, tiled=True)[0]
    own_live = live[me].reshape(-1)
    kern = kernels[0, 0].reshape(-1, 2 * Q * SUB).astype(jnp.float32)
    kern_v = kern[:, : Q * SUB].reshape(-1, Q, SUB)
    kern_u = kern[:, Q * SUB :].reshape(-1, Q, SUB)
    order = np.zeros((SUB, 2, 4, steps), np.float32)
    for h, residues in enumerate(((1, 2, 3, 0), (7, 6, 5, 4))):
        for g, r in enumerate(residues):
            order[RADIX * np.arange(steps) + r, h, g, np.arange(steps)] = 1.0
    kern_u = jnp.einsum("mqu,uw->mqw", kern_u, order.reshape(SUB, SUB), precision=HIGH)
    noise = weights[0, 0].reshape(-1, Q, Q).astype(jnp.float32) * own_live[:, None, None]
    section = jnp.einsum("mqv,mcvu->mcqu", kern_v, patch, precision=HIGH)
    sampled = jnp.einsum("mcqu,mru->mcqr", section, kern_u, precision=HIGH) * noise[:, None]
    again = jnp.einsum("mqv,mcqr->mcvr", kern_v, sampled, precision=HIGH)
    regridded = jnp.einsum("mcvr,mru->mcvu", again, kern_u, precision=HIGH)
    spread = lax.all_gather(regridded, "tile").reshape(-1, group, 2, SUB, 2, 4, steps)
    if group == count:
        added = scatter_patches((places[0][0], places[1][0]), spread[0])
    else:
        added = lax.fori_loop(
            0,
            count // group,
            lambda i, sofar: sofar + scatter_patches((places[0][i], places[1][i]), spread[i]),
            jnp.zeros((4, slab, 2 * part), jnp.float32),
        )

    here = here.astype(jnp.float32) * (64.0 * tops)[:, None, None]
    here = here.reshape(RADIX, part, 2 * columns)
    turned = fold_complex(
        [here[j, :, :columns] for j in range(RADIX)], [here[j, :, columns:] for j in range(RADIX)]
    )
    turned = jnp.stack([jnp.concatenate(z, axis=0) for z in turned])
    grid = jnp.einsum("rop,rpu->rou", table, turned, precision=HIGH).reshape(RADIX, 2, part, columns)
    spec_v, spec_u = spectrum[0, 0], spectrum[0, 1]
    v_plus, v_minus = by_residue(spec_v), by_residue(mirror(spec_v))

    def to_list(values):
        by = by_residue(values)
        return jnp.concatenate([by[1], by[2], by[3], by[0, : part // 2], by[4, : part // 2]])

    edge = spec_u[0], spec_u[length // 2]
    packed = 3 * part
    flat = jnp.full((1,), (edge[0] + edge[1]) * 0.25)
    u_plus = lax.dynamic_update_slice(to_list(spec_u), flat, (packed,))
    u_minus = lax.dynamic_update_slice(to_list(mirror(spec_u)), flat, (packed,))
    u_plus = lax.dynamic_slice_in_dim(u_plus, me * columns, columns)
    u_minus = lax.dynamic_slice_in_dim(u_minus, me * columns, columns)
    prior = v_plus[:, :, None] * u_plus + v_minus[:, :, None] * u_minus
    spot = packed % columns
    lone = grid[:, :, :, spot]
    flip = jnp.concatenate([mirror(lone[:1]), lone[:0:-1, :, ::-1]])
    cross = (v_plus + v_minus) * ((edge[0] - edge[1]) * 0.25)
    flip = flip * cross[:, None] * jnp.array([1.0, -1.0], jnp.float32)[None, :, None]
    chosen = (jnp.arange(columns) == spot) & (me == packed // columns)
    gridded = grid * prior[:, None] + jnp.where(chosen, flip[..., None], 0.0)
    back = jnp.einsum(
        "rop,rou->rpu", table, gridded.reshape(RADIX, 2 * part, columns), precision=HIGH
    )
    back = fold_complex([back[r, :part] for r in range(RADIX)], [-back[r, part:] for r in range(RADIX)])
    crest = jnp.max(tops) * (length * (length / 2048.0) ** 1.5 * 32.0)
    column = jnp.concatenate([jnp.concatenate([z[0], -z[1]], axis=-1) for z in back])
    reply = (column * (1.0 / crest)).astype(jnp.float16).reshape(devices, slab, 2 * columns)
    line = lax.all_to_all(reply, "tile", split_axis=0, concat_axis=0, tiled=True)

    line = line.reshape(4, fine_split, slab, 2, columns).transpose(0, 2, 3, 1, 4)
    line = line.reshape(4, slab, 2 * part).astype(jnp.float32) * crest
    lines = jnp.einsum("gyo,gop->gyp", line, across, precision=HIGH) + added
    z = [(lines[r, :, :part], lines[r, :, part:]) for r in range(3)]
    lines = unfold_real(lines[3, :, :part], lines[3, :, part:], z)
    image = jnp.concatenate(lines, axis=-1) * (1.0 / float(length * length))

    own = jnp.stack(
        [
            jnp.sum(rows_now * rows_now),
            jnp.sum(field * image),
            jnp.sum(rows_now * image),
            jnp.sum(image * image),
        ]
    )
    total = lax.psum(own, ("chan", "tile"))
    alpha = total[0] / total[1]
    fresh = total[0] - 2.0 * alpha * total[2] + alpha * alpha * total[3]
    new_rows = rows_now - alpha * image
    new_field = new_rows + fresh / total[0] * field
    return (new_rows[None], new_field[None])


def solution(mesh):
    placed = (
        P("chan", "tile", None),
        P("chan", "tile", None),
        P("chan", "tile", None, None),
        P("chan", "tile", None, None, None),
        P("chan", "tile", None, None, None),
        P("chan", None, None),
    )
    return jax.shard_map(
        body,
        mesh=mesh,
        in_specs=placed,
        out_specs=(P("chan", "tile", None), P("chan", "tile", None)),
        check_vma=False,
    )
```

```python
import math

import jax
import jax.numpy as jnp
import numpy as np
from jax import lax
from jax.sharding import PartitionSpec as P

SUB = 64
Q = 64
RADIX = 8
HIGH = lax.Precision.HIGH
ROOT = 0.5**0.5


def phase_table(left, right, length):
    angle = 2.0 * math.pi / length * (np.outer(left, right) % length)
    return np.cos(angle), np.sin(angle)


def full_tables(length):
    part = length // RADIX
    index = np.arange(part)
    blocks = []
    for r in range(RADIX):
        co, si = phase_table(RADIX * index + r, index, length)
        blocks.append(np.block([[co, si], [-si, co]]))
    return np.stack(blocks).astype(np.float32)


def row_tables(length, table):
    part = length // RADIX
    index = np.arange(part)
    half = np.arange(part // 2)
    last = np.zeros((2, 2, part // 2, 2, part), np.float32)
    for place, r in enumerate((0, RADIX // 2)):
        co, si = phase_table(RADIX * half + r, index, length)
        low = -si
        if r == 0:
            low[0] = 1.0 - 2.0 * (index % 2)
        last[0, place, :, place] = co
        last[1, place, :, place] = low
    return np.concatenate([table[1:4], last.reshape(1, 2 * part, 2 * part)])


def fold_real(x):
    s04, d04, s26, d26 = x[0] + x[4], x[0] - x[4], x[2] + x[6], x[2] - x[6]
    s15, d15, s37, d37 = x[1] + x[5], x[1] - x[5], x[3] + x[7], x[3] - x[7]
    even, odd = s04 + s26, s15 + s37
    minus, plus = (d15 - d37) * ROOT, (d15 + d37) * ROOT
    return (
        (even + odd, None),
        (d04 + minus, -d26 - plus),
        (s04 - s26, s37 - s15),
        (d04 - minus, d26 - plus),
        (even - odd, None),
    )


def fold_complex(re, im):
    left, right = fold_real(re), fold_real(im)
    out = [(left[0][0], right[0][0])]
    for r in (1, 2, 3):
        out.append((left[r][0] - right[r][1], left[r][1] + right[r][0]))
    out.append((left[4][0], right[4][0]))
    for r in (3, 2, 1):
        out.append((left[r][0] + right[r][1], right[r][0] - left[r][1]))
    return out


def unfold_real(z0, z4, z):
    (a1, b1), (a2, b2), (a3, b3) = z
    even, odd = z0 + z4, z0 - z4
    sa, da, sb, db = a1 + a3, a1 - a3, b1 + b3, b1 - b3
    return (
        even + sa + a2,
        odd + (da - sb) * ROOT - b2,
        even - db - a2,
        odd - (da + sb) * ROOT + b2,
        even - sa + a2,
        odd - (da - sb) * ROOT - b2,
        even + db - a2,
        odd + (da + sb) * ROOT + b2,
    )


def mirror(values):
    return jnp.roll(values[..., ::-1], 1, axis=-1)


def by_residue(values):
    return values.reshape(-1, RADIX).T


def body(residual, direction, cover, kernels, weights, spectrum):
    rows_now = residual[0]
    field = direction[0]
    devices = lax.axis_size("tile")
    me = lax.axis_index("tile")
    slab, length = field.shape
    part = length // RADIX
    columns = length // 2 // devices
    tile_cols = length // SUB // devices
    tile_count = (length // SUB) * tile_cols
    table = full_tables(length)
    across = row_tables(length, table)

    folded = fold_real([field[:, j * part : (j + 1) * part] for j in range(RADIX)])
    rows = jnp.stack(
        [jnp.concatenate(folded[r], axis=-1) for r in (1, 2, 3)]
        + [jnp.concatenate([folded[0][0], folded[4][0]], axis=-1)]
    )
    top = jnp.maximum(jnp.max(jnp.abs(field)), 1e-30)
    listed = cover[0, 0].astype(jnp.float32).reshape(-1)
    facts = lax.all_gather(jnp.concatenate([listed, top[None]]), "tile")
    tops = facts[:, -1]
    sent = jnp.einsum("gyp,gop->gyo", rows, across, precision=HIGH)
    sent = (sent * (1.0 / (64.0 * top))).astype(jnp.float16)
    fine_split = devices // 4
    sent = sent.reshape(4, slab, 2, fine_split, columns).transpose(0, 3, 1, 2, 4)
    sent = sent.reshape(devices, slab, 2 * columns)
    here = lax.all_to_all(sent, "tile", split_axis=0, concat_axis=0, tiled=True)

    listing = jnp.swapaxes(facts[:, :-1].astype(jnp.int32).reshape((devices,) + cover.shape[2:]), 0, 1)
    count = listing.size
    group = count if devices <= 4 else count // devices
    owner = lax.broadcasted_iota(jnp.int32, listing.shape, 1)
    live = (listing < tile_count).astype(jnp.float32)
    safe = jnp.minimum(listing, tile_count - 1)
    tile_a = (safe // tile_cols).reshape(-1)
    tile_b = (owner * tile_cols + safe % tile_cols).reshape(-1)
    period = length // SUB

    def turn(index, position):
        angle = (2.0 * math.pi / period) * ((index[:, None] * position) % period).astype(jnp.float32)
        return jnp.cos(angle), jnp.sin(angle)

    steps = SUB // RADIX
    spots = np.arange(part)
    offset = (RADIX * np.arange(steps)[None, :] + np.arange(RADIX)[:, None]).reshape(-1)
    inner = phase_table(spots, offset, length)
    inner_re = inner[0].astype(np.float32).reshape(part, RADIX, steps).transpose(1, 0, 2)[:, :, None]
    inner_im = inner[1].astype(np.float32).reshape(part, RADIX, steps).transpose(1, 0, 2)[:, :, None]
    rows_at = me * slab + jnp.arange(slab, dtype=jnp.int32)
    fine = (jnp.arange(SUB, dtype=jnp.int32)[:, None] * rows_at[None]) % length
    fine_angle = (2.0 * math.pi / length) * fine.astype(jnp.float32)
    fine_re, fine_im = jnp.cos(fine_angle)[None], jnp.sin(fine_angle)[None]

    def along_table(tile_b):
        base_re, base_im = turn(tile_b, jnp.arange(part, dtype=jnp.int32)[None])
        base_re, base_im = base_re.T[None, :, :, None], base_im.T[None, :, :, None]
        along_re = (inner_re * base_re - inner_im * base_im).reshape(RADIX, part, group * steps)
        along_im = (inner_re * base_im + inner_im * base_re).reshape(RADIX, part, group * steps)
        nought = jnp.zeros_like(along_re[0])

        def block(first, second, turned):
            sign = -1.0 if turned else 1.0
            upper = jnp.concatenate([first, -second], axis=-1)
            return jnp.concatenate([upper, sign * jnp.concatenate([second, first], axis=-1)])

        groups = []
        for r in (1, 2, 3):
            s = RADIX - r
            groups.append(
                jnp.concatenate(
                    [block(along_re[r], along_im[r], False), block(along_re[s], along_im[s], True)],
                    axis=-1,
                )
            )
        upper = jnp.concatenate([along_re[0], -along_im[0], nought, nought], axis=-1)
        lower = jnp.concatenate([nought, nought, along_re[4], -along_im[4]], axis=-1)
        groups.append(jnp.concatenate([upper, lower]))
        return jnp.stack(groups)

    def down_table(tile_a):
        step_re, step_im = turn(tile_a, rows_at[None])
        step_re, step_im = step_re[:, None], step_im[:, None]
        down_re = fine_re * step_re - fine_im * step_im
        down_im = fine_re * step_im + fine_im * step_re
        down = jnp.stack(
            [jnp.stack([down_re, down_im], axis=2), jnp.stack([-down_im, down_re], axis=2)], axis=1
        )
        return down

    def gather_patches(where):
        strip = jnp.einsum("gyp,gpo->gyo", rows, along_table(where[1]), precision=HIGH)
        strip = strip.reshape(4, slab, 2, 2, group, steps)
        return jnp.einsum("movpy,gyhpmt->movhgt", down_table(where[0]), strip, precision=HIGH)

    def scatter_patches(where, spread):
        lifted = jnp.einsum("movpy,movhgt->gyhpmt", down_table(where[0]), spread, precision=HIGH)
        lifted = lifted.reshape(4, slab, 4 * group * steps)
        return jnp.einsum("gyo,gpo->gyp", lifted, along_table(where[1]), precision=HIGH)

    places = (tile_a.reshape(-1, group), tile_b.reshape(-1, group))
    if group == count:
        partial = gather_patches((places[0][0], places[1][0]))
    else:
        partial = lax.map(gather_patches, places)
    partial = partial.reshape(devices, count // devices, 2, SUB, SUB)
    patch = lax.psum_scatter(partial, "tile", scatter_dimension=0, tiled=True)[0]
    own_live = live[me].reshape(-1)
    kern = kernels[0, 0].reshape(-1, 2 * Q * SUB).astype(jnp.float32)
    kern_v = kern[:, : Q * SUB].reshape(-1, Q, SUB)
    kern_u = kern[:, Q * SUB :].reshape(-1, Q, SUB)
    order = np.zeros((SUB, 2, 4, steps), np.float32)
    for h, residues in enumerate(((1, 2, 3, 0), (7, 6, 5, 4))):
        for g, r in enumerate(residues):
            order[RADIX * np.arange(steps) + r, h, g, np.arange(steps)] = 1.0
    kern_u = jnp.einsum("mqu,uw->mqw", kern_u, order.reshape(SUB, SUB), precision=HIGH)
    noise = weights[0, 0].reshape(-1, Q, Q).astype(jnp.float32) * own_live[:, None, None]
    section = jnp.einsum("mqv,mcvu->mcqu", kern_v, patch, precision=HIGH)
    sampled = jnp.einsum("mcqu,mru->mcqr", section, kern_u, precision=HIGH) * noise[:, None]
    again = jnp.einsum("mqv,mcqr->mcvr", kern_v, sampled, precision=HIGH)
    regridded = jnp.einsum("mcvr,mru->mcvu", again, kern_u, precision=HIGH)
    if devices <= 4:
        ring = [regridded]
        for k in range(1, devices):
            pairs = [(i, (i + k) % devices) for i in range(devices)]
            ring.append(lax.ppermute(regridded, "tile", pairs))
        here, regridded = lax.optimization_barrier((here, regridded))
        twice = jnp.stack(ring[::-1] * 2)
        spread = lax.dynamic_slice_in_dim(twice, devices - 1 - me, devices)
    else:
        spread = lax.all_gather(regridded, "tile")
    spread = spread.reshape(-1, group, 2, SUB, 2, 4, steps)
    if group == count:
        added = scatter_patches((places[0][0], places[1][0]), spread[0])
    else:
        added = lax.fori_loop(
            0,
            count // group,
            lambda i, sofar: sofar + scatter_patches((places[0][i], places[1][i]), spread[i]),
            jnp.zeros((4, slab, 2 * part), jnp.float32),
        )

    here = here.astype(jnp.float32) * (64.0 * tops)[:, None, None]
    here = here.reshape(RADIX, part, 2 * columns)
    turned = fold_complex(
        [here[j, :, :columns] for j in range(RADIX)], [here[j, :, columns:] for j in range(RADIX)]
    )
    turned = jnp.stack([jnp.concatenate(z, axis=0) for z in turned])
    grid = jnp.einsum("rop,rpu->rou", table, turned, precision=HIGH).reshape(RADIX, 2, part, columns)
    spec_v, spec_u = spectrum[0, 0], spectrum[0, 1]
    v_plus, v_minus = by_residue(spec_v), by_residue(mirror(spec_v))

    def to_list(values):
        by = by_residue(values)
        return jnp.concatenate([by[1], by[2], by[3], by[0, : part // 2], by[4, : part // 2]])

    edge = spec_u[0], spec_u[length // 2]
    packed = 3 * part
    flat = jnp.full((1,), (edge[0] + edge[1]) * 0.25)
    u_plus = lax.dynamic_update_slice(to_list(spec_u), flat, (packed,))
    u_minus = lax.dynamic_update_slice(to_list(mirror(spec_u)), flat, (packed,))
    u_plus = lax.dynamic_slice_in_dim(u_plus, me * columns, columns)
    u_minus = lax.dynamic_slice_in_dim(u_minus, me * columns, columns)
    prior = v_plus[:, :, None] * u_plus + v_minus[:, :, None] * u_minus
    spot = packed % columns
    lone = grid[:, :, :, spot]
    flip = jnp.concatenate([mirror(lone[:1]), lone[:0:-1, :, ::-1]])
    cross = (v_plus + v_minus) * ((edge[0] - edge[1]) * 0.25)
    flip = flip * cross[:, None] * jnp.array([1.0, -1.0], jnp.float32)[None, :, None]
    chosen = (jnp.arange(columns) == spot) & (me == packed // columns)
    gridded = grid * prior[:, None] + jnp.where(chosen, flip[..., None], 0.0)
    back = jnp.einsum(
        "rop,rou->rpu", table, gridded.reshape(RADIX, 2 * part, columns), precision=HIGH
    )
    back = fold_complex([back[r, :part] for r in range(RADIX)], [-back[r, part:] for r in range(RADIX)])
    crest = jnp.max(tops) * (length * (length / 2048.0) ** 1.5 * 32.0)
    column = jnp.concatenate([jnp.concatenate([z[0], -z[1]], axis=-1) for z in back])
    reply = (column * (1.0 / crest)).astype(jnp.float16).reshape(devices, slab, 2 * columns)
    line = lax.all_to_all(reply, "tile", split_axis=0, concat_axis=0, tiled=True)

    line = line.reshape(4, fine_split, slab, 2, columns).transpose(0, 2, 3, 1, 4)
    line = line.reshape(4, slab, 2 * part).astype(jnp.float32) * crest
    lines = jnp.einsum("gyo,gop->gyp", line, across, precision=HIGH) + added
    z = [(lines[r, :, :part], lines[r, :, part:]) for r in range(3)]
    lines = unfold_real(lines[3, :, :part], lines[3, :, part:], z)
    image = jnp.concatenate(lines, axis=-1) * (1.0 / float(length * length))

    own = jnp.stack(
        [
            jnp.sum(rows_now * rows_now),
            jnp.sum(field * image),
            jnp.sum(rows_now * image),
            jnp.sum(image * image),
        ]
    )
    total = lax.psum(lax.psum(own, "tile"), "chan")
    alpha = total[0] / total[1]
    fresh = total[0] - 2.0 * alpha * total[2] + alpha * alpha * total[3]
    new_rows = rows_now - alpha * image
    new_field = new_rows + fresh / total[0] * field
    return (new_rows[None], new_field[None])


def solution(mesh):
    placed = (
        P("chan", "tile", None),
        P("chan", "tile", None),
        P("chan", "tile", None, None),
        P("chan", "tile", None, None, None),
        P("chan", "tile", None, None, None),
        P("chan", None, None),
    )
    return jax.shard_map(
        body,
        mesh=mesh,
        in_specs=placed,
        out_specs=(P("chan", "tile", None), P("chan", "tile", None)),
        check_vma=False,
    )
```
